32 devices in a mesh: row: 8 (over y, x, core), col: 4 (over z).
Axes of the slice: x: 2, y: 2, z: 4, core: 2. Of those that a mesh axis runs over, the one named last changes fastest.
Arguments:
- matrix: float32 [8192, 2048], P('row', 'col'), may hold values from -100 to 100, as said below
Outputs:
- updated: float32 [8192, 2048], P('row', 'col')
- top: float32 [128, 2048], P(None, 'col')
The draws below stay inside these ranges and needn't reach their ends.
Inputs may be any that keep to these rules, and one draw needn't show every extreme that they name: The first 128 columns of matrix have full column rank.
All inputs are finite; a program needn't handle non-finite values.
Results may differ from the reference program's by a relative error of at most 0.0006.
Values sent between devices are 32-bit elements; how exact they have to be, the bound alone decides.
A program may use at most 64 MiB of HBM per device.

```python
import math
import jax
import jax.numpy as jnp
from jax import lax

B = 128
ROWS = 8192
COLS = 2048


def draw_matrix(key, part):
    key_base = jax.random.fold_in(key, 0)
    key_rows = jax.random.fold_in(key, 1)
    key_cols = jax.random.fold_in(key, 2)
    key_left = jax.random.fold_in(key, 4)
    key_right = jax.random.fold_in(key, 5)
    rise = 1.0 + 2.0 * jnp.arange(ROWS, dtype=jnp.float32)[:, None] / ROWS
    col_scale = jnp.exp(jax.random.uniform(key_cols, (1, COLS), jnp.float32, 0.0, math.log(4.0)))
    noise = jnp.clip(jax.random.normal(key_base, (ROWS, COLS), jnp.float32), -6.0, 6.0)
    base = noise
    row_scale = jnp.exp(jax.random.uniform(key_rows, (ROWS, 1), jnp.float32, 0.0, math.log(4.0)))
    left = jnp.clip(jax.random.normal(key_left, (ROWS, 4), jnp.float32), -2.5, 2.5)
    right = jnp.clip(jax.random.normal(key_right, (4, COLS), jnp.float32), -2.5, 2.5)
    shared = left[:, 0:1] * right[0:1, :] + left[:, 1:2] * right[1:2, :]
    shared = shared + left[:, 2:3] * right[2:3, :] + left[:, 3:4] * right[3:4, :]
    near = 0.125 * shared + 0.0025 * noise
    in_panel = jnp.arange(COLS)[None, :] < B
    mixed = jnp.where(in_panel, near, base)
    return 0.25 * mixed * row_scale * col_scale * rise


def setup_inputs(seed: int = 0) -> dict:
    arg_keys = jax.random.split(jax.random.key(seed), 2)
    matrix = draw_matrix(jax.random.fold_in(arg_keys[1], 71), 0)
    return dict(matrix=matrix)


def matmul(left, right):
    return jnp.dot(left.astype(jnp.float32), right.astype(jnp.float32), precision=lax.Precision.HIGHEST, preferred_element_type=jnp.float32)

def project(left, right):
    return jnp.einsum('rb,rc->bc', left, right, precision=lax.Precision.HIGHEST)

def factor_once(block, gram_mat):
    lower = jnp.linalg.cholesky(gram_mat)
    identity = jnp.eye(block.shape[1], dtype=jnp.float32)
    inverse = jax.scipy.linalg.solve_triangular(lower, identity, lower=True)
    return (matmul(block, inverse.T), lower.T)

def factor_twice(block):
    first_q, first_r = factor_once(block, project(block, block))
    second_q, second_r = factor_once(first_q, project(first_q, first_q))
    return (second_q, matmul(second_r, first_r))

def reference(matrix):
    panel = matrix[:, :B]
    basis, upper = factor_twice(panel)
    coeffs = project(basis, matrix)
    updated = matrix - matmul(basis, coeffs)
    scale = math.sqrt(ROWS)
    updated = jnp.concatenate([basis * scale, updated[:, B:]], 1)
    return (updated, coeffs / scale)
```

```python
import functools
import math

import jax
import jax.numpy as jnp
from jax import lax
from jax.experimental import pallas as pl
from jax.experimental.pallas import tpu as pltpu
from jax.sharding import PartitionSpec as P

B = 128
S = 8
CHUNKS = 8
HI = lax.Precision.HIGHEST


def mm(left, right, dims):
    return lax.dot_general(
        left, right, (dims, ((), ())), precision=HI, preferred_element_type=jnp.float32
    )


def factor_steps(w_ref, low, high):
    lane = lax.broadcasted_iota(jnp.int32, (S, B), 1)
    sub = lax.broadcasted_iota(jnp.int32, (S, B), 0)
    wide = lax.broadcasted_iota(jnp.int32, (B, B), 1)

    def step(k, carry):
        w = w_ref[...]
        rows = w[:S]
        d = {}
        for i in range(S):
            for j in range(i + 1):
                d[i, j] = jnp.broadcast_to(rows[i : i + 1, j : j + 1], (S, B))
        rows = jnp.where(lane < S, jnp.where(lane == sub, 1.0, 0.0), rows)
        p = [jnp.broadcast_to(rows[j : j + 1], (S, B)) for j in range(S)]
        t = None
        for j in range(S):
            inv = lax.rsqrt(d[j, j])
            l = {i: d[i, j] * inv for i in range(j + 1, S)}
            for i in range(j + 1, S):
                for m in range(j + 1, i + 1):
                    d[i, m] = d[i, m] - l[i] * l[m]
            tj = p[j] * inv
            for i in range(j + 1, S):
                p[i] = p[i] - l[i] * tj
            t = tj if t is None else jnp.where(sub == j, tj, t)
        mult = jnp.where((lane >= S) & (lane < B - S * k), t, 0.0)
        t = pltpu.roll(t, B - S, 1)
        rest = pltpu.roll(jnp.where(wide < S, 0.0, w), B - S, 1)
        rest = rest - mm(mult, t, ((0,), (0,)))
        w_ref[: B - S] = rest[S:]
        w_ref[B - S :] = t
        return carry

    lax.fori_loop(low, high, step, 0)


class Sum:
    def __init__(self, size, me, src, box, full, sems):
        self.size, self.me, self.src, self.box, self.full = size, me, src, box, full
        self.sems = sems
        self.slab = max(8, B // size)
        self.owners = B // self.slab

    def rows(self, owner):
        return pl.ds(pl.multiple_of(owner * self.slab, self.slab), self.slab)

    def own(self, device, what):
        if self.owners == self.size:
            what()
        else:
            pl.when(device < self.owners)(what)

    def scatter_copy(self, i):
        peer = self.me ^ i
        return pltpu.make_async_remote_copy(
            src_ref=self.src.at[self.rows(peer)],
            dst_ref=self.box.at[i],
            send_sem=self.sems.at[0, i],
            recv_sem=self.sems.at[1, i],
            device_id={"row": peer},
            device_id_type=pl.DeviceIdType.MESH,
        )

    def scatter_from(self, i):
        return pltpu.make_async_remote_copy(
            src_ref=self.box.at[i],
            dst_ref=self.box.at[i],
            send_sem=self.sems.at[0, i],
            recv_sem=self.sems.at[1, i],
            device_id={"row": self.me ^ i},
            device_id_type=pl.DeviceIdType.MESH,
        )

    def gather_copy(self, i, owner):
        return pltpu.make_async_remote_copy(
            src_ref=self.full.at[self.rows(owner)],
            dst_ref=self.full.at[self.rows(owner)],
            send_sem=self.sems.at[2, i],
            recv_sem=self.sems.at[3, i],
            device_id={"row": self.me ^ i},
            device_id_type=pl.DeviceIdType.MESH,
        )

    def start(self):
        for i in range(1, self.size):
            self.own(self.me ^ i, lambda: self.scatter_copy(i).start())

    def middle(self):
        for i in range(1, self.size):
            self.own(self.me ^ i, lambda: self.scatter_copy(i).wait_send())

        def add():
            total = self.src[self.rows(self.me)]
            for i in range(1, self.size):
                self.scatter_from(i).wait_recv()
                total = total + self.box[i]
            self.full[self.rows(self.me)] = total
            for i in range(1, self.size):
                self.gather_copy(i, self.me).start()

        self.own(self.me, add)

    def end(self):
        for i in range(1, self.size):
            self.own(self.me ^ i, lambda: self.gather_copy(i, self.me ^ i).wait_recv())

    def drain(self):
        def sent():
            for i in range(1, self.size):
                self.gather_copy(i, self.me).wait_send()

        self.own(self.me, sent)


def kernel(
    nrow, ncol, m_hbm, out_hbm, top_ref,
    m_v, a_v, q_v, o_v, s1_v, s2_v, sp_v, g1_v, g2_v, p_v, box1, box2, boxp,
    in_sems, out_sems, chain_sems, g_sems, sems1, sems2, semsp,
):
    me = lax.axis_index("row")
    z = lax.axis_index("col")
    height, width = m_v.shape
    part = height // CHUNKS
    load_m = pltpu.make_async_copy(m_hbm, m_v, in_sems.at[0])
    load_a = pltpu.make_async_copy(m_hbm.at[:, pl.ds(0, B)], a_v, in_sems.at[1])

    @pl.when(z == 0)
    def _():
        load_a.start()

    load_m.start()

    barrier = pltpu.get_barrier_semaphore()
    for i in range(1, nrow):
        pl.semaphore_signal(
            barrier, inc=1, device_id={"row": me ^ i}, device_id_type=pl.DeviceIdType.MESH
        )
    for i in range(1, ncol):
        pl.semaphore_signal(
            barrier, inc=1, device_id={"col": z ^ i}, device_id_type=pl.DeviceIdType.MESH
        )

    @pl.when(z == 0)
    def _():
        load_a.wait()
        s1_v[...] = mm(a_v[...], a_v[...], ((0,), (0,)))

    pl.semaphore_wait(barrier, nrow + ncol - 2)

    def chain(c):
        block = a_v.at[pl.ds(c * part, part)]
        return pltpu.make_async_remote_copy(
            src_ref=block,
            dst_ref=block,
            send_sem=chain_sems.at[0, c],
            recv_sem=chain_sems.at[1, c],
            device_id={"col": lax.rem(z + 1, ncol)},
            device_id_type=pl.DeviceIdType.MESH,
        )

    def hand(i):
        return pltpu.make_async_remote_copy(
            src_ref=g1_v,
            dst_ref=g1_v,
            send_sem=g_sems.at[0, i],
            recv_sem=g_sems.at[1, 0],
            device_id={"col": i},
            device_id_type=pl.DeviceIdType.MESH,
        )

    @pl.when(z == 0)
    def _():
        first = Sum(nrow, me, s1_v, box1, g1_v, sems1)
        first.start()
        for c in range(CHUNKS):
            chain(c).start()
        first.middle()
        first.end()
        first.drain()
        factor_steps(g1_v, 0, B // S)
        for i in range(1, ncol):
            hand(i).start()

    @pl.when(z > 0)
    def _():
        for c in range(CHUNKS):
            chain(c).wait_recv()

            @pl.when(z < ncol - 1)
            def _():
                chain(c).start()

        hand(0).wait_recv()

    load_m.wait()
    for c in range(CHUNKS):
        rows = pl.ds(c * part, part)
        q_v[rows] = mm(a_v[rows], g1_v[...], ((1,), (1,)))
    q = q_v[...]
    s2_v[...] = mm(q, q, ((0,), (0,)))
    second = Sum(nrow, me, s2_v, box2, g2_v, sems2)
    second.start()
    coeffs = Sum(nrow, me, sp_v, boxp, p_v, semsp)
    sp_v[...] = mm(q_v[...], m_v[...], ((0,), (0,)))
    coeffs.start()
    second.middle()
    second.end()
    second.drain()
    factor_steps(g2_v, 0, B // S // 2)
    coeffs.middle()
    factor_steps(g2_v, B // S // 2, B // S)
    coeffs.end()
    coeffs.drain()

    scale = math.sqrt(height * nrow)
    g2 = g2_v[...]
    on_panel = z == 0
    for c in range(width // B):
        cols = pl.ds(c * B, B)
        part_c = mm(g2, p_v[:, cols], ((1,), (0,)))
        top_ref[:, cols] = part_c / scale
        back = mm(g2, part_c, ((0,), (0,)))
        if c == 0:
            back = jnp.where(on_panel, -scale * g2.T, back)
        p_v[:, cols] = back

    def store(c):
        rows = pl.ds(c * part, part)
        return pltpu.make_async_copy(o_v.at[rows], out_hbm.at[rows], out_sems.at[c])

    for c in range(CHUNKS):
        rows = pl.ds(c * part, part)
        change = mm(q_v[rows], p_v[...], ((1,), (0,)))
        base = m_v[rows]
        o_v[rows, :B] = jnp.where(on_panel, 0.0, base[:, :B]) - change[:, :B]
        o_v[rows, B:] = base[:, B:] - change[:, B:]
        store(c).start()
    for c in range(CHUNKS):
        store(c).wait()

    @pl.when(z < ncol - 1)
    def _():
        for c in range(CHUNKS):
            chain(c).wait_send()

    @pl.when(z == 0)
    def _():
        for i in range(1, ncol):
            hand(i).wait_send()


def on_device(nrow, ncol, matrix):
    height, width = matrix.shape
    slab = max(8, B // nrow)
    f32 = jnp.float32
    dma = pltpu.SemaphoreType.DMA
    return pl.pallas_call(
        functools.partial(kernel, nrow, ncol),
        out_shape=(
            jax.ShapeDtypeStruct((height, width), f32),
            jax.ShapeDtypeStruct((B, width), f32),
        ),
        in_specs=[pl.BlockSpec(memory_space=pl.ANY)],
        out_specs=(
            pl.BlockSpec(memory_space=pl.ANY),
            pl.BlockSpec(memory_space=pltpu.VMEM),
        ),
        scratch_shapes=[
            pltpu.VMEM((height, width), f32),
            pltpu.VMEM((height, B), f32),
            pltpu.VMEM((height, B), f32),
            pltpu.VMEM((height, width), f32),
            pltpu.VMEM((B, B), f32),
            pltpu.VMEM((B, B), f32),
            pltpu.VMEM((B, width), f32),
            pltpu.VMEM((B, B), f32),
            pltpu.VMEM((B, B), f32),
            pltpu.VMEM((B, width), f32),
            pltpu.VMEM((nrow, slab, B), f32),
            pltpu.VMEM((nrow, slab, B), f32),
            pltpu.VMEM((nrow, slab, width), f32),
            dma((2,)),
            dma((CHUNKS,)),
            dma((2, CHUNKS)),
            dma((2, ncol)),
            dma((4, nrow)),
            dma((4, nrow)),
            dma((4, nrow)),
        ],
        compiler_params=pltpu.CompilerParams(
            collective_id=0, has_side_effects=True, vmem_limit_bytes=40 * 2**20
        ),
    )(matrix)


def solution(mesh):
    nrow, ncol = mesh.shape["row"], mesh.shape["col"]
    return jax.shard_map(
        functools.partial(on_device, nrow, ncol),
        mesh=mesh,
        in_specs=(P("row", "col"),),
        out_specs=(P("row", "col"), P(None, "col")),
        check_vma=False,
    )
```

```python
import functools
import math

import jax
import jax.numpy as jnp
from jax import lax
from jax.experimental import pallas as pl
from jax.experimental.pallas import tpu as pltpu
from jax.sharding import PartitionSpec as P

B = 128
S = 8
CHUNKS = 8
HI = lax.Precision.HIGHEST


def mm(left, right, dims):
    return lax.dot_general(
        left, right, (dims, ((), ())), precision=HI, preferred_element_type=jnp.float32
    )


def factor_steps(w_ref, low, high, state=None):
    lane = lax.broadcasted_iota(jnp.int32, (S, B), 1)
    sub = lax.broadcasted_iota(jnp.int32, (S, B), 0)
    wide = lax.broadcasted_iota(jnp.int32, (B - 2 * S, B), 1)

    def step(k, state):
        rows, mult, last = state
        d = {}
        for j in range(S):
            column = jnp.broadcast_to(rows[:, j : j + 1], (S, B))
            for i in range(j, S):
                d[i, j] = jnp.broadcast_to(column[i : i + 1], (S, B))
        rest = w_ref[S : B - S] - mm(mult, last, ((0,), (0,)))[2 * S :]
        rest = pltpu.roll(jnp.where(wide < S, 0.0, rest), B - S, 1)
        w_ref[: B - 2 * S] = rest
        w_ref[B - 2 * S : B - S] = pltpu.roll(jnp.where(lane < S, 0.0, last), B - S, 1)
        rows = jnp.where(lane < S, jnp.where(lane == sub, 1.0, 0.0), rows)
        p = [jnp.broadcast_to(rows[j : j + 1], (S, B)) for j in range(S)]
        t = None
        for j in range(S):
            inv = lax.rsqrt(d[j, j])
            l = {i: d[i, j] * inv for i in range(j + 1, S)}
            for i in range(j + 1, S):
                for m in range(j + 1, i + 1):
                    d[i, m] = d[i, m] - l[i] * l[m]
            tj = p[j] * inv
            for i in range(j + 1, S):
                p[i] = p[i] - l[i] * tj
            t = tj if t is None else jnp.where(sub == j, tj, t)
        mult = jnp.where((lane >= S) & (lane < B - S * k), t, 0.0)
        last = pltpu.roll(t, B - S, 1)
        after = rest[:S]
        for i in range(S):
            column = jnp.broadcast_to(mult[:, S + i : S + i + 1], (S, B))
            drop = jnp.sum(column * last, axis=0, keepdims=True)
            after = jnp.where(sub == i, after - drop, after)
        return after, mult, last

    if low == 0:
        state = (w_ref[:S], jnp.zeros((S, B), jnp.float32), w_ref[B - S :])
    state = lax.fori_loop(low, high, step, state)
    if high == B // S:
        w_ref[B - S :] = state[2]
    return state


class Sum:
    def __init__(self, size, me, src, box, full, sems):
        self.size, self.me, self.src, self.box, self.full = size, me, src, box, full
        self.sems = sems
        self.slab = max(8, B // size)
        self.owners = B // self.slab

    def rows(self, owner):
        return pl.ds(pl.multiple_of(owner * self.slab, self.slab), self.slab)

    def own(self, device, what):
        if self.owners == self.size:
            what()
        else:
            pl.when(device < self.owners)(what)

    def scatter_copy(self, i):
        peer = self.me ^ i
        return pltpu.make_async_remote_copy(
            src_ref=self.src.at[self.rows(peer)],
            dst_ref=self.box.at[i],
            send_sem=self.sems.at[0, i],
            recv_sem=self.sems.at[1, i],
            device_id={"row": peer},
            device_id_type=pl.DeviceIdType.MESH,
        )

    def scatter_from(self, i):
        return pltpu.make_async_remote_copy(
            src_ref=self.box.at[i],
            dst_ref=self.box.at[i],
            send_sem=self.sems.at[0, i],
            recv_sem=self.sems.at[1, i],
            device_id={"row": self.me ^ i},
            device_id_type=pl.DeviceIdType.MESH,
        )

    def gather_copy(self, i, owner):
        return pltpu.make_async_remote_copy(
            src_ref=self.full.at[self.rows(owner)],
            dst_ref=self.full.at[self.rows(owner)],
            send_sem=self.sems.at[2, i],
            recv_sem=self.sems.at[3, i],
            device_id={"row": self.me ^ i},
            device_id_type=pl.DeviceIdType.MESH,
        )

    def start(self):
        for i in range(1, self.size):
            self.own(self.me ^ i, lambda: self.scatter_copy(i).start())

    def middle(self):
        for i in range(1, self.size):
            self.own(self.me ^ i, lambda: self.scatter_copy(i).wait_send())

        def add():
            total = self.src[self.rows(self.me)]
            for i in range(1, self.size):
                self.scatter_from(i).wait_recv()
                total = total + self.box[i]
            self.full[self.rows(self.me)] = total

        self.own(self.me, add)

    def spread(self):
        def send():
            for i in range(1, self.size):
                self.gather_copy(i, self.me).start()

        self.own(self.me, send)

    def end(self):
        for i in range(1, self.size):
            self.own(self.me ^ i, lambda: self.gather_copy(i, self.me ^ i).wait_recv())

    def drain(self):
        def sent():
            for i in range(1, self.size):
                self.gather_copy(i, self.me).wait_send()

        self.own(self.me, sent)


def kernel(
    nrow, ncol, m_hbm, q_v, g2_v, p_v,
    m_v, a_v, s1_v, s2_v, sp_v, g1_v, box1, box2, boxp,
    in_sems, chain_sems, g_sems, sems1, sems2, semsp,
):
    me = lax.axis_index("row")
    z = lax.axis_index("col")
    height = m_v.shape[0]
    part = height // CHUNKS
    load_m = pltpu.make_async_copy(m_hbm, m_v, in_sems.at[0])
    load_a = pltpu.make_async_copy(m_hbm.at[:, pl.ds(0, B)], a_v, in_sems.at[1])

    barrier = pltpu.get_barrier_semaphore()
    for i in range(1, nrow):
        pl.semaphore_signal(
            barrier, inc=1, device_id={"row": me ^ i}, device_id_type=pl.DeviceIdType.MESH
        )
    for i in range(1, ncol):
        pl.semaphore_signal(
            barrier, inc=1, device_id={"col": z ^ i}, device_id_type=pl.DeviceIdType.MESH
        )

    @pl.when(z == 0)
    def _():
        load_a.start()
        load_a.wait()
        s1_v[...] = mm(a_v[...], a_v[...], ((0,), (0,)))

    load_m.start()
    pl.semaphore_wait(barrier, nrow + ncol - 2)

    def chain(c):
        block = a_v.at[pl.ds(c * part, part)]
        return pltpu.make_async_remote_copy(
            src_ref=block,
            dst_ref=block,
            send_sem=chain_sems.at[0, c],
            recv_sem=chain_sems.at[1, c],
            device_id={"col": lax.rem(z + 1, ncol)},
            device_id_type=pl.DeviceIdType.MESH,
        )

    def forward(c):
        chain(c).wait_recv()
        pl.when(z < ncol - 1)(lambda: chain(c).start())

    first = Sum(nrow, me, s1_v, box1, g1_v, sems1)
    slab = g1_v.at[first.rows(me)]

    def hand(i):
        return pltpu.make_async_remote_copy(
            src_ref=slab,
            dst_ref=slab,
            send_sem=g_sems.at[0, i],
            recv_sem=g_sems.at[1, 0],
            device_id={"col": i},
            device_id_type=pl.DeviceIdType.MESH,
        )

    @pl.when(z == 0)
    def _():
        first.start()
        for c in range(2):
            chain(c).start()
        first.middle()

        def give():
            for i in range(1, ncol):
                hand(i).start()

        first.own(me, give)
        for c in range(2, CHUNKS):
            chain(c).start()

    @pl.when(z > 0)
    def _():
        forward(0)
        forward(1)
        first.own(me, lambda: hand(0).wait_recv())

    first.spread()
    first.end()
    first.drain()

    @pl.when(z == 0)
    def _():
        def given():
            for i in range(1, ncol):
                hand(i).wait_send()

        first.own(me, given)

    state = None
    for low, chunks in ((0, (2, 3)), (4, (4, 5)), (8, (6, 7)), (12, ())):
        state = factor_steps(g1_v, low, low + 4, state)
        for c in chunks:
            pl.when(z > 0)(functools.partial(forward, c))

    for c in range(CHUNKS):
        rows = pl.ds(c * part, part)
        q_v[rows] = mm(a_v[rows], g1_v[...], ((1,), (1,)))
    q = q_v[...]
    s2_v[...] = mm(q, q, ((0,), (0,)))
    second = Sum(nrow, me, s2_v, box2, g2_v, sems2)
    second.start()
    load_m.wait()
    coeffs = Sum(nrow, me, sp_v, boxp, p_v, semsp)
    sp_v[...] = mm(q_v[...], m_v[...], ((0,), (0,)))
    coeffs.start()
    second.middle()
    second.spread()
    second.end()
    second.drain()
    state = factor_steps(g2_v, 0, B // S // 2)
    coeffs.middle()
    coeffs.spread()
    factor_steps(g2_v, B // S // 2, B // S, state)
    coeffs.end()
    coeffs.drain()

    @pl.when(z < ncol - 1)
    def _():
        for c in range(CHUNKS):
            chain(c).wait_send()


def project_kernel(rows, m_ref, q_ref, g2_ref, p_ref, out_ref, top_ref, back_v):
    width = m_ref.shape[1]
    scale = math.sqrt(rows)
    on_panel = lax.axis_index("col") == 0

    @pl.when(pl.program_id(0) == 0)
    def _():
        g2 = g2_ref[...]
        c = mm(g2, p_ref[...], ((1,), (0,)))
        top_ref[...] = c / scale
        back = mm(g2, c, ((0,), (0,)))
        back_v[:, :B] = jnp.where(on_panel, -scale * g2.T, back[:, :B])
        back_v[:, B:] = back[:, B:]

    change = mm(q_ref[...], back_v[...], ((1,), (0,)))
    base = m_ref[...]
    out_ref[:, :B] = jnp.where(on_panel, 0.0, base[:, :B]) - change[:, :B]
    out_ref[:, B:] = base[:, B:] - change[:, B:]


def on_device(nrow, ncol, matrix):
    height, width = matrix.shape
    slab = max(8, B // nrow)
    f32 = jnp.float32
    dma = pltpu.SemaphoreType.DMA
    shape = jax.ShapeDtypeStruct
    basis, inverse, coeffs = pl.pallas_call(
        functools.partial(kernel, nrow, ncol),
        out_shape=(shape((height, B), f32), shape((B, B), f32), shape((B, width), f32)),
        in_specs=[pl.BlockSpec(memory_space=pl.ANY)],
        out_specs=(pl.BlockSpec(memory_space=pltpu.VMEM),) * 3,
        scratch_shapes=[
            pltpu.VMEM((height, width), f32),
            pltpu.VMEM((height, B), f32),
            pltpu.VMEM((B, B), f32),
            pltpu.VMEM((B, B), f32),
            pltpu.VMEM((B, width), f32),
            pltpu.VMEM((B, B), f32),
            pltpu.VMEM((nrow, slab, B), f32),
            pltpu.VMEM((nrow, slab, B), f32),
            pltpu.VMEM((nrow, slab, width), f32),
            dma((2,)),
            dma((2, CHUNKS)),
            dma((2, ncol)),
            dma((4, nrow)),
            dma((4, nrow)),
            dma((4, nrow)),
        ],
        compiler_params=pltpu.CompilerParams(
            collective_id=0, has_side_effects=True, vmem_limit_bytes=60 * 2**20
        ),
    )(matrix)
    part = height // 4
    whole = pl.BlockSpec(memory_space=pltpu.VMEM)
    return pl.pallas_call(
        functools.partial(project_kernel, height * nrow),
        grid=(height // part,),
        out_shape=(shape((height, width), f32), shape((B, width), f32)),
        in_specs=[
            pl.BlockSpec((part, width), lambda i: (i, 0)),
            pl.BlockSpec((part, B), lambda i: (i, 0)),
            whole,
            whole,
        ],
        out_specs=(
            pl.BlockSpec((part, width), lambda i: (i, 0)),
            pl.BlockSpec((B, width), lambda i: (0, 0)),
        ),
        scratch_shapes=[pltpu.VMEM((B, width), f32)],
        compiler_params=pltpu.CompilerParams(vmem_limit_bytes=60 * 2**20),
    )(matrix, basis, inverse, coeffs)


def solution(mesh):
    nrow, ncol = mesh.shape["row"], mesh.shape["col"]
    return jax.shard_map(
        functools.partial(on_device, nrow, ncol),
        mesh=mesh,
        in_specs=(P("row", "col"),),
        out_specs=(P("row", "col"), P(None, "col")),
        check_vma=False,
    )
```

```python
import functools
import math

import jax
import jax.numpy as jnp
from jax import lax
from jax.experimental import pallas as pl
from jax.experimental.pallas import tpu as pltpu
from jax.sharding import PartitionSpec as P

B = 128
S = 8
CHUNKS = 8
HI = lax.Precision.HIGHEST


def mm(left, right, dims):
    return lax.dot_general(
        left, right, (dims, ((), ())), precision=HI, preferred_element_type=jnp.float32
    )


def factor_steps(w_ref, low, high, state=None, after_step=None):
    lane = lax.broadcasted_iota(jnp.int32, (S, B), 1)
    sub = lax.broadcasted_iota(jnp.int32, (S, B), 0)
    wide = lax.broadcasted_iota(jnp.int32, (B - 2 * S, B), 1)

    def step(k, state):
        rows, mult, last = state
        d = {}
        for j in range(S):
            column = jnp.broadcast_to(rows[:, j : j + 1], (S, B))
            for i in range(j, S):
                d[i, j] = jnp.broadcast_to(column[i : i + 1], (S, B))
        rest = w_ref[S : B - S] - mm(mult, last, ((0,), (0,)))[2 * S :]
        rest = pltpu.roll(jnp.where(wide < S, 0.0, rest), B - S, 1)
        w_ref[: B - 2 * S] = rest
        w_ref[B - 2 * S : B - S] = pltpu.roll(jnp.where(lane < S, 0.0, last), B - S, 1)
        rows = jnp.where(lane < S, jnp.where(lane == sub, 1.0, 0.0), rows)
        p = [jnp.broadcast_to(rows[j : j + 1], (S, B)) for j in range(S)]
        t = None
        for j in range(S):
            inv = lax.rsqrt(d[j, j])
            l = {i: d[i, j] * inv for i in range(j + 1, S)}
            for i in range(j + 1, S):
                for m in range(j + 1, i + 1):
                    d[i, m] = d[i, m] - l[i] * l[m]
            tj = p[j] * inv
            for i in range(j + 1, S):
                p[i] = p[i] - l[i] * tj
            t = tj if t is None else jnp.where(sub == j, tj, t)
        mult = jnp.where((lane >= S) & (lane < B - S * k), t, 0.0)
        last = pltpu.roll(t, B - S, 1)
        after = rest[:S]
        for i in range(S):
            column = jnp.broadcast_to(mult[:, S + i : S + i + 1], (S, B))
            drop = jnp.sum(column * last, axis=0, keepdims=True)
            after = jnp.where(sub == i, after - drop, after)
        if after_step is not None:
            after_step(k)
        return after, mult, last

    if low == 0:
        state = (w_ref[:S], jnp.zeros((S, B), jnp.float32), w_ref[B - S :])
    state = lax.fori_loop(low, high, step, state)
    if high == B // S:
        w_ref[B - S :] = state[2]
    return state


class Sum:
    def __init__(self, size, me, src, box, full, sems):
        self.size, self.me, self.src, self.box, self.full = size, me, src, box, full
        self.sems = sems
        self.slab = max(8, B // size)
        self.owners = B // self.slab

    def rows(self, owner):
        return pl.ds(pl.multiple_of(owner * self.slab, self.slab), self.slab)

    def own(self, device, what):
        if self.owners == self.size:
            what()
        else:
            pl.when(device < self.owners)(what)

    def scatter_copy(self, i):
        peer = self.me ^ i
        return pltpu.make_async_remote_copy(
            src_ref=self.src.at[self.rows(peer)],
            dst_ref=self.box.at[i],
            send_sem=self.sems.at[0, i],
            recv_sem=self.sems.at[1, i],
            device_id={"row": peer},
            device_id_type=pl.DeviceIdType.MESH,
        )

    def scatter_from(self, i):
        return pltpu.make_async_remote_copy(
            src_ref=self.box.at[i],
            dst_ref=self.box.at[i],
            send_sem=self.sems.at[0, i],
            recv_sem=self.sems.at[1, i],
            device_id={"row": self.me ^ i},
            device_id_type=pl.DeviceIdType.MESH,
        )

    def gather_copy(self, i, owner):
        return pltpu.make_async_remote_copy(
            src_ref=self.full.at[self.rows(owner)],
            dst_ref=self.full.at[self.rows(owner)],
            send_sem=self.sems.at[2, i],
            recv_sem=self.sems.at[3, i],
            device_id={"row": self.me ^ i},
            device_id_type=pl.DeviceIdType.MESH,
        )

    def start(self):
        for i in range(1, self.size):
            self.own(self.me ^ i, lambda: self.scatter_copy(i).start())

    def middle(self):
        for i in range(1, self.size):
            self.own(self.me ^ i, lambda: self.scatter_copy(i).wait_send())

        def add():
            total = self.src[self.rows(self.me)]
            for i in range(1, self.size):
                self.scatter_from(i).wait_recv()
                total = total + self.box[i]
            self.full[self.rows(self.me)] = total
            self.box[0] = total

        self.own(self.me, add)

    def spread(self):
        def send():
            for i in range(1, self.size):
                self.gather_copy(i, self.me).start()

        self.own(self.me, send)

    def end(self):
        for i in range(1, self.size):
            self.own(self.me ^ i, lambda: self.gather_copy(i, self.me ^ i).wait_recv())

    def drain(self):
        def sent():
            for i in range(1, self.size):
                self.gather_copy(i, self.me).wait_send()

        self.own(self.me, sent)


def kernel(
    nrow, ncol, m_hbm, q_v, g2_v, p_v,
    m_v, a_v, s1_v, s2_v, sp_v, g1_v, box1, box2, boxp,
    in_sems, chain_sems, g_sems, sems1, sems2, semsp,
):
    me = lax.axis_index("row")
    z = lax.axis_index("col")
    height = m_v.shape[0]
    part = height // CHUNKS
    load_m = pltpu.make_async_copy(m_hbm, m_v, in_sems.at[0])
    load_a = pltpu.make_async_copy(m_hbm.at[:, pl.ds(0, B)], a_v, in_sems.at[1])

    barrier = pltpu.get_barrier_semaphore()
    for i in range(1, nrow):
        pl.semaphore_signal(
            barrier, inc=1, device_id={"row": me ^ i}, device_id_type=pl.DeviceIdType.MESH
        )
    for i in range(1, ncol):
        pl.semaphore_signal(
            barrier, inc=1, device_id={"col": z ^ i}, device_id_type=pl.DeviceIdType.MESH
        )

    pl.when(z == 0)(load_a.start)
    load_m.start()
    pl.semaphore_wait(barrier, nrow + ncol - 2)

    def chain(c):
        block = a_v.at[pl.ds(pl.multiple_of(c * part, part), part)]
        return pltpu.make_async_remote_copy(
            src_ref=block,
            dst_ref=block,
            send_sem=chain_sems.at[0, c],
            recv_sem=chain_sems.at[1, c],
            device_id={"col": lax.rem(z + 1, ncol)},
            device_id_type=pl.DeviceIdType.MESH,
        )

    passes_on = (z > 0) & (z < ncol - 1)

    def forward(c):
        chain(c).wait_recv()
        chain(c).start()

    first = Sum(nrow, me, s1_v, box1, g1_v, sems1)
    second = Sum(nrow, me, s2_v, box2, g2_v, sems2)
    coeffs = Sum(nrow, me, sp_v, boxp, p_v, semsp)

    def hand(which, total, i):
        return pltpu.make_async_remote_copy(
            src_ref=total.box.at[0],
            dst_ref=total.full.at[total.rows(me)],
            send_sem=g_sems.at[2 * which, i],
            recv_sem=g_sems.at[2 * which + 1, 0],
            device_id={"col": i},
            device_id_type=pl.DeviceIdType.MESH,
        )

    def give(which, total):
        def send():
            for i in range(1, ncol):
                hand(which, total, i).start()

        first.own(me, send)

    @pl.when(z == 0)
    def _():
        load_a.wait()
        for c in range(3):
            chain(c).start()
        s1_v[...] = mm(a_v[...], a_v[...], ((0,), (0,)))
        first.start()
        first.middle()
        give(0, first)
        first.spread()
        for c in range(3, CHUNKS):
            chain(c).start()

    @pl.when(passes_on)
    def _():
        for c in range(4):
            forward(c)

    @pl.when(z > 0)
    def _():
        first.own(me, lambda: hand(0, first, 0).wait_recv())
        first.spread()

    first.end()
    first.drain()

    def pass_on(k):
        @pl.when(passes_on & (k % 3 == 1) & (k < 12))
        def _():
            forward(4 + k // 3)

    factor_steps(g1_v, 0, B // S, None, pass_on)

    big = 2 * part

    @pl.when(z == 0)
    def _():
        for c in range(CHUNKS // 2):
            rows = pl.ds(c * big, big)
            q_v[rows] = mm(a_v[rows], g1_v[...], ((1,), (1,)))
        q = q_v[...]
        s2_v[...] = mm(q, q, ((0,), (0,)))
        second.start()
        load_m.wait()
        sp_v[...] = mm(q_v[...], m_v[...], ((0,), (0,)))
        second.middle()
        give(1, second)
        second.spread()
        coeffs.start()

    @pl.when(z > 0)
    def _():
        load_m.wait()
        for c in range(CHUNKS // 2):

            @pl.when(z == ncol - 1)
            def _():
                chain(2 * c).wait_recv()
                chain(2 * c + 1).wait_recv()

            rows = pl.ds(c * big, big)
            q = mm(a_v[rows], g1_v[...], ((1,), (1,)))
            q_v[rows] = q
            term = mm(q, m_v[rows], ((0,), (0,)))
            if c == 0:
                sp_v[...] = term
            else:
                sp_v[...] += term
        coeffs.start()
        second.own(me, lambda: hand(1, second, 0).wait_recv())
        second.spread()

    second.end()
    second.drain()
    state = factor_steps(g2_v, 0, B // S // 2)
    coeffs.middle()
    coeffs.spread()
    factor_steps(g2_v, B // S // 2, B // S, state)
    coeffs.end()
    coeffs.drain()

    @pl.when(z == 0)
    def _():
        def given():
            for i in range(1, ncol):
                hand(0, first, i).wait_send()
                hand(1, second, i).wait_send()

        first.own(me, given)

    @pl.when(z < ncol - 1)
    def _():
        for c in range(CHUNKS):
            chain(c).wait_send()


def halves(x):
    high = x.astype(jnp.bfloat16)
    return high, (x - high.astype(jnp.float32)).astype(jnp.bfloat16)


def project_kernel(rows, m_ref, q_ref, g2_ref, p_ref, out_ref, top_ref, back_v):
    width = m_ref.shape[1]
    scale = math.sqrt(rows)
    on_panel = lax.axis_index("col") == 0

    @pl.when(pl.program_id(0) == 0)
    def _():
        g2 = g2_ref[...]
        c = mm(g2, p_ref[...], ((1,), (0,)))
        top_ref[...] = c / scale
        back = mm(g2, c, ((0,), (0,)))
        leading = jnp.where(on_panel, -scale * g2.T, back[:, :B])
        high, low = halves(jnp.concatenate([leading, back[:, B:]], 1))
        back_v[:B] = high
        back_v[B : 2 * B] = high
        back_v[2 * B :] = low

    high, low = halves(q_ref[...])
    change = jnp.dot(
        jnp.concatenate([high, low, high], 1), back_v[...], preferred_element_type=jnp.float32
    )
    base = m_ref[...]
    out_ref[:, :B] = jnp.where(on_panel, 0.0, base[:, :B]) - change[:, :B]
    out_ref[:, B:] = base[:, B:] - change[:, B:]


def on_device(nrow, ncol, matrix):
    height, width = matrix.shape
    slab = max(8, B // nrow)
    f32 = jnp.float32
    dma = pltpu.SemaphoreType.DMA
    shape = jax.ShapeDtypeStruct
    basis, inverse, coeffs = pl.pallas_call(
        functools.partial(kernel, nrow, ncol),
        out_shape=(shape((height, B), f32), shape((B, B), f32), shape((B, width), f32)),
        in_specs=[pl.BlockSpec(memory_space=pl.ANY)],
        out_specs=(pl.BlockSpec(memory_space=pltpu.VMEM),) * 3,
        scratch_shapes=[
            pltpu.VMEM((height, width), f32),
            pltpu.VMEM((height, B), f32),
            pltpu.VMEM((B, B), f32),
            pltpu.VMEM((B, B), f32),
            pltpu.VMEM((B, width), f32),
            pltpu.VMEM((B, B), f32),
            pltpu.VMEM((nrow, slab, B), f32),
            pltpu.VMEM((nrow, slab, B), f32),
            pltpu.VMEM((nrow, slab, width), f32),
            dma((2,)),
            dma((2, CHUNKS)),
            dma((4, ncol)),
            dma((4, nrow)),
            dma((4, nrow)),
            dma((4, nrow)),
        ],
        compiler_params=pltpu.CompilerParams(
            collective_id=0, has_side_effects=True, vmem_limit_bytes=60 * 2**20
        ),
    )(matrix)
    part = height // 4
    whole = pl.BlockSpec(memory_space=pltpu.VMEM)
    return pl.pallas_call(
        functools.partial(project_kernel, height * nrow),
        grid=(height // part,),
        out_shape=(shape((height, width), f32), shape((B, width), f32)),
        in_specs=[
            pl.BlockSpec((part, width), lambda i: (i, 0)),
            pl.BlockSpec((part, B), lambda i: (i, 0)),
            whole,
            whole,
        ],
        out_specs=(
            pl.BlockSpec((part, width), lambda i: (i, 0)),
            pl.BlockSpec((B, width), lambda i: (0, 0)),
        ),
        scratch_shapes=[pltpu.VMEM((3 * B, width), jnp.bfloat16)],
        compiler_params=pltpu.CompilerParams(vmem_limit_bytes=60 * 2**20),
    )(matrix, basis, inverse, coeffs)


def solution(mesh):
    nrow, ncol = mesh.shape["row"], mesh.shape["col"]
    return jax.shard_map(
        functools.partial(on_device, nrow, ncol),
        mesh=mesh,
        in_specs=(P("row", "col"),),
        out_specs=(P("row", "col"), P(None, "col")),
        check_vma=False,
    )
```

```python
import functools
import math

import jax
import jax.numpy as jnp
from jax import lax
from jax.experimental import pallas as pl
from jax.experimental.pallas import tpu as pltpu
from jax.sharding import PartitionSpec as P

B = 128
S = 8
CHUNKS = 8
HI = lax.Precision.HIGHEST


def mm(left, right, dims):
    return lax.dot_general(
        left, right, (dims, ((), ())), precision=HI, preferred_element_type=jnp.float32
    )


def factor_steps(w_ref, low, high, state=None, after_step=None):
    lane = lax.broadcasted_iota(jnp.int32, (S, B), 1)
    sub = lax.broadcasted_iota(jnp.int32, (S, B), 0)
    wide = lax.broadcasted_iota(jnp.int32, (B - 2 * S, B), 1)

    def step(k, state):
        rows, mult, last = state
        d = {}
        for j in range(S):
            column = jnp.broadcast_to(rows[:, j : j + 1], (S, B))
            for i in range(j, S):
                d[i, j] = jnp.broadcast_to(column[i : i + 1], (S, B))
        rest = w_ref[S : B - S] - mm(mult, last, ((0,), (0,)))[2 * S :]
        rest = pltpu.roll(jnp.where(wide < S, 0.0, rest), B - S, 1)
        w_ref[: B - 2 * S] = rest
        w_ref[B - 2 * S : B - S] = pltpu.roll(jnp.where(lane < S, 0.0, last), B - S, 1)
        rows = jnp.where(lane < S, jnp.where(lane == sub, 1.0, 0.0), rows)
        p = [jnp.broadcast_to(rows[j : j + 1], (S, B)) for j in range(S)]
        t = None
        for j in range(S):
            inv = lax.rsqrt(d[j, j])
            l = {i: d[i, j] * inv for i in range(j + 1, S)}
            for i in range(j + 1, S):
                for m in range(j + 1, i + 1):
                    d[i, m] = d[i, m] - l[i] * l[m]
            tj = p[j] * inv
            for i in range(j + 1, S):
                p[i] = p[i] - l[i] * tj
            t = tj if t is None else jnp.where(sub == j, tj, t)
        mult = jnp.where((lane >= S) & (lane < B - S * k), t, 0.0)
        last = pltpu.roll(t, B - S, 1)
        after = rest[:S]
        for i in range(S):
            column = jnp.broadcast_to(mult[:, S + i : S + i + 1], (S, B))
            drop = jnp.sum(column * last, axis=0, keepdims=True)
            after = jnp.where(sub == i, after - drop, after)
        if after_step is not None:
            after_step(k)
        return after, mult, last

    if low == 0:
        state = (w_ref[:S], jnp.zeros((S, B), jnp.float32), w_ref[B - S :])
    state = lax.fori_loop(low, high, step, state)
    if high == B // S:
        w_ref[B - S :] = state[2]
    return state


class Sum:
    def __init__(self, size, me, src, box, full, sems):
        self.size, self.me, self.src, self.box, self.full = size, me, src, box, full
        self.sems = sems
        self.slab = max(8, B // size)
        self.owners = B // self.slab

    def rows(self, owner):
        return pl.ds(pl.multiple_of(owner * self.slab, self.slab), self.slab)

    def own(self, device, what):
        if self.owners == self.size:
            what()
        else:
            pl.when(device < self.owners)(what)

    def scatter_copy(self, i):
        peer = self.me ^ i
        return pltpu.make_async_remote_copy(
            src_ref=self.src.at[self.rows(peer)],
            dst_ref=self.box.at[i],
            send_sem=self.sems.at[0, i],
            recv_sem=self.sems.at[1, i],
            device_id={"row": peer},
            device_id_type=pl.DeviceIdType.MESH,
        )

    def scatter_from(self, i):
        return pltpu.make_async_remote_copy(
            src_ref=self.box.at[i],
            dst_ref=self.box.at[i],
            send_sem=self.sems.at[0, i],
            recv_sem=self.sems.at[1, i],
            device_id={"row": self.me ^ i},
            device_id_type=pl.DeviceIdType.MESH,
        )

    def gather_copy(self, i, owner):
        return pltpu.make_async_remote_copy(
            src_ref=self.full.at[self.rows(owner)],
            dst_ref=self.full.at[self.rows(owner)],
            send_sem=self.sems.at[2, i],
            recv_sem=self.sems.at[3, i],
            device_id={"row": self.me ^ i},
            device_id_type=pl.DeviceIdType.MESH,
        )

    def start(self):
        for i in range(1, self.size):
            self.own(self.me ^ i, lambda: self.scatter_copy(i).start())

    def middle(self):
        for i in range(1, self.size):
            self.own(self.me ^ i, lambda: self.scatter_copy(i).wait_send())

        def add():
            total = self.src[self.rows(self.me)]
            for i in range(1, self.size):
                self.scatter_from(i).wait_recv()
                total = total + self.box[i]
            self.full[self.rows(self.me)] = total
            self.box[0] = total

        self.own(self.me, add)

    def spread(self):
        def send():
            for i in range(1, self.size):
                self.gather_copy(i, self.me).start()

        self.own(self.me, send)

    def end(self):
        for i in range(1, self.size):
            self.own(self.me ^ i, lambda: self.gather_copy(i, self.me ^ i).wait_recv())

    def drain(self):
        def sent():
            for i in range(1, self.size):
                self.gather_copy(i, self.me).wait_send()

        self.own(self.me, sent)


def kernel(
    nrow, ncol, m_hbm, q_v, g2_v, p_v,
    m_v, a_v, s1_v, s2_v, sp_v, g1_v, box1, box2, boxp,
    in_sems, chain_sems, g_sems, sems1, sems2, semsp,
):
    me = lax.axis_index("row")
    z = lax.axis_index("col")
    height = m_v.shape[0]
    part = height // CHUNKS
    load_m = pltpu.make_async_copy(m_hbm, m_v, in_sems.at[0])
    load_a = pltpu.make_async_copy(m_hbm.at[:, pl.ds(0, B)], a_v, in_sems.at[1])

    barrier = pltpu.get_barrier_semaphore()
    for i in range(1, nrow):
        pl.semaphore_signal(
            barrier, inc=1, device_id={"row": me ^ i}, device_id_type=pl.DeviceIdType.MESH
        )
    for i in range(1, ncol):
        pl.semaphore_signal(
            barrier, inc=1, device_id={"col": z ^ i}, device_id_type=pl.DeviceIdType.MESH
        )

    pl.when(z == 0)(load_a.start)
    load_m.start()
    pl.semaphore_wait(barrier, nrow + ncol - 2)

    def chain(c):
        block = a_v.at[pl.ds(pl.multiple_of(c * part, part), part)]
        return pltpu.make_async_remote_copy(
            src_ref=block,
            dst_ref=block,
            send_sem=chain_sems.at[0, c],
            recv_sem=chain_sems.at[1, c],
            device_id={"col": lax.rem(z + 1, ncol)},
            device_id_type=pl.DeviceIdType.MESH,
        )

    passes_on = (z > 0) & (z < ncol - 1)

    def forward(c):
        chain(c).wait_recv()
        chain(c).start()

    first = Sum(nrow, me, s1_v, box1, g1_v, sems1)
    second = Sum(nrow, me, s2_v, box2, g2_v, sems2)
    coeffs = Sum(nrow, me, sp_v, boxp, p_v, semsp)

    def hand(which, total, i):
        return pltpu.make_async_remote_copy(
            src_ref=total.box.at[0],
            dst_ref=total.full.at[total.rows(me)],
            send_sem=g_sems.at[2 * which, i],
            recv_sem=g_sems.at[2 * which + 1, 0],
            device_id={"col": i},
            device_id_type=pl.DeviceIdType.MESH,
        )

    def give(which, total):
        def send():
            for i in range(1, ncol):
                hand(which, total, i).start()

        first.own(me, send)

    @pl.when(z == 0)
    def _():
        load_a.wait()
        for c in range(3):
            chain(c).start()
        s1_v[...] = mm(a_v[...], a_v[...], ((0,), (0,)))
        first.start()
        first.middle()
        give(0, first)
        first.spread()
        for c in range(3, CHUNKS):
            chain(c).start()

    @pl.when(passes_on)
    def _():
        for c in range(4):
            forward(c)

    @pl.when(z > 0)
    def _():
        first.own(me, lambda: hand(0, first, 0).wait_recv())
        first.spread()

    first.end()
    first.drain()

    def pass_on(k):
        @pl.when(passes_on & (k % 3 == 1) & (k < 12))
        def _():
            forward(4 + k // 3)

    factor_steps(g1_v, 0, B // S, None, pass_on)

    big = 2 * part

    @pl.when(z == 0)
    def _():
        for c in range(CHUNKS // 2):
            rows = pl.ds(c * big, big)
            q_v[rows] = mm(a_v[rows], g1_v[...], ((1,), (1,)))
        q = q_v[...]
        s2_v[...] = mm(q, q, ((0,), (0,)))
        second.start()
        load_m.wait()
        sp_v[...] = mm(q_v[...], m_v[...], ((0,), (0,)))
        second.middle()
        give(1, second)
        second.spread()
        coeffs.start()

    @pl.when(z > 0)
    def _():
        load_m.wait()
        for c in range(CHUNKS // 2):
            if c == CHUNKS // 2 - 1:
                second.own(me, lambda: hand(1, second, 0).wait_recv())
                second.spread()

            @pl.when(z == ncol - 1)
            def _():
                chain(2 * c).wait_recv()
                chain(2 * c + 1).wait_recv()

            rows = pl.ds(c * big, big)
            q = mm(a_v[rows], g1_v[...], ((1,), (1,)))
            q_v[rows] = q
            term = mm(q, m_v[rows], ((0,), (0,)))
            if c == 0:
                sp_v[...] = term
            else:
                sp_v[...] += term
        coeffs.start()

    second.end()
    second.drain()
    state = factor_steps(g2_v, 0, B // S // 2)
    coeffs.middle()
    coeffs.spread()
    factor_steps(g2_v, B // S // 2, B // S, state)
    coeffs.end()
    coeffs.drain()

    @pl.when(z == 0)
    def _():
        def given():
            for i in range(1, ncol):
                hand(0, first, i).wait_send()
                hand(1, second, i).wait_send()

        first.own(me, given)

    @pl.when(z < ncol - 1)
    def _():
        for c in range(CHUNKS):
            chain(c).wait_send()


def halves(x):
    high = x.astype(jnp.bfloat16)
    return high, (x - high.astype(jnp.float32)).astype(jnp.bfloat16)


def project_kernel(rows, m_ref, q_ref, g2_ref, p_ref, out_hbm, top_ref, out_v, back_v, sems):
    height, width = m_ref.shape
    part = height // 4
    scale = math.sqrt(rows)
    on_panel = lax.axis_index("col") == 0
    g2 = g2_ref[...]
    c = mm(g2, p_ref[...], ((1,), (0,)))
    top_ref[...] = c / scale
    back = mm(g2, c, ((0,), (0,)))
    leading = jnp.where(on_panel, -scale * g2.T, back[:, :B])
    high, low = halves(jnp.concatenate([leading, back[:, B:]], 1))
    back_v[:B] = high
    back_v[B : 2 * B] = high
    back_v[2 * B :] = low

    def store(i):
        block = pl.ds(i * part, part)
        return pltpu.make_async_copy(out_v.at[block], out_hbm.at[block], sems.at[i])

    for i in range(4):
        block = pl.ds(i * part, part)
        high, low = halves(q_ref[block])
        change = jnp.dot(
            jnp.concatenate([high, low, high], 1), back_v[...], preferred_element_type=jnp.float32
        )
        base = m_ref[block]
        out_v[block, :B] = jnp.where(on_panel, 0.0, base[:, :B]) - change[:, :B]
        out_v[block, B:] = base[:, B:] - change[:, B:]
        store(i).start()
    for i in range(4):
        store(i).wait()


def on_device(nrow, ncol, matrix):
    height, width = matrix.shape
    slab = max(8, B // nrow)
    f32 = jnp.float32
    dma = pltpu.SemaphoreType.DMA
    shape = jax.ShapeDtypeStruct
    basis, inverse, coeffs = pl.pallas_call(
        functools.partial(kernel, nrow, ncol),
        out_shape=(shape((height, B), f32), shape((B, B), f32), shape((B, width), f32)),
        in_specs=[pl.BlockSpec(memory_space=pl.ANY)],
        out_specs=(pl.BlockSpec(memory_space=pltpu.VMEM),) * 3,
        scratch_shapes=[
            pltpu.VMEM((height, width), f32),
            pltpu.VMEM((height, B), f32),
            pltpu.VMEM((B, B), f32),
            pltpu.VMEM((B, B), f32),
            pltpu.VMEM((B, width), f32),
            pltpu.VMEM((B, B), f32),
            pltpu.VMEM((nrow, slab, B), f32),
            pltpu.VMEM((nrow, slab, B), f32),
            pltpu.VMEM((nrow, slab, width), f32),
            dma((2,)),
            dma((2, CHUNKS)),
            dma((4, ncol)),
            dma((4, nrow)),
            dma((4, nrow)),
            dma((4, nrow)),
        ],
        compiler_params=pltpu.CompilerParams(
            collective_id=0, has_side_effects=True, vmem_limit_bytes=60 * 2**20
        ),
    )(matrix)
    whole = pl.BlockSpec(memory_space=pltpu.VMEM)
    return pl.pallas_call(
        functools.partial(project_kernel, height * nrow),
        out_shape=(shape((height, width), f32), shape((B, width), f32)),
        in_specs=[whole] * 4,
        out_specs=(pl.BlockSpec(memory_space=pl.ANY), whole),
        scratch_shapes=[
            pltpu.VMEM((height, width), f32),
            pltpu.VMEM((3 * B, width), jnp.bfloat16),
            dma((4,)),
        ],
        compiler_params=pltpu.CompilerParams(vmem_limit_bytes=32 * 2**20),
    )(matrix, basis, inverse, coeffs)


def solution(mesh):
    nrow, ncol = mesh.shape["row"], mesh.shape["col"]
    return jax.shard_map(
        functools.partial(on_device, nrow, ncol),
        mesh=mesh,
        in_specs=(P("row", "col"),),
        out_specs=(P("row", "col"), P(None, "col")),
        check_vma=False,
    )
```
